256 devices in a mesh: row: 16 (over z_hi, y), col: 16 (over z_lo, x, core).
Axes of the slice: x: 4, y: 4, z: 8 (z_hi: 4, z_lo: 2; z = z_hi * 2 + z_lo), core: 2. Of those that a mesh axis runs over, the one named last changes fastest.
Arguments:
- hidden_act: bfloat16 [768, 26624], P('col', 'row'), may hold values from -6 to 6
- out_grad: bfloat16 [768, 16384], P('row', 'col'), may hold values from -6 to 6
- down_weight: bfloat16 [26624, 16384], P('row', 'col'), may hold values from -0.046875 to 0.046875
Outputs:
- fisher: float32 [26624, 16384], P('row', 'col')
- hidden_grad: bfloat16 [768, 26624], P('col', 'row')
The draws below stay inside these ranges and needn't reach their ends.
All inputs are finite; a program needn't handle non-finite values.
Results may differ from the reference program's by a relative error of at most 0.001.
Values may be sent and summed in bfloat16 or wider, within the bound.
A program may use at most 64 MiB of HBM per device.

```python
import jax
import jax.numpy as jnp
from jax import lax

D = 16384
FFW = 26624
SEQ = 96
EXAMPLES = 8
TOKENS = 768


def spiked(result, rng, source, target, parts, factor):
    owner, partner = [(jnp.arange(result.shape[dim]) // (result.shape[dim] // parts)).reshape([-1 if axis == dim else 1 for axis in range(result.ndim)]) for dim in (source, target)]
    chosen = jax.random.permutation(rng, parts)[partner]
    strong = (owner == chosen) | (owner == (partner + parts // 2) % parts)
    return jnp.where(strong, factor * result, result)


def block_levels(own_key, shape, pieces, smallest, top_value):
    gain, own = 1.0, jax.random.fold_in(own_key, 6)
    for position, parts in pieces:
        draws = jnp.exp(jax.random.uniform(jax.random.fold_in(own, position), (parts,), jnp.float32, smallest / len(pieces), top_value / len(pieces)))
        gain = gain * jnp.repeat(draws, shape[position] // parts).reshape([-1 if axis == position else 1 for axis in range(len(shape))])
    return gain


def gaussian(own_key, shape, width, reach, split=(), kind=jnp.bfloat16):
    drawn = jax.random.normal(own_key, shape, jnp.float32) * width
    if len(split) > 0:
        drawn = block_levels(own_key, shape, split, -0.22, 0.18) * drawn
    return jnp.clip(drawn, min=-reach, max=reach).astype(kind)


def gaussian_with(stream_key, extent, scale, reach, pieces, heavy, dtype=jnp.bfloat16):
    drawn = scale * jax.random.normal(stream_key, extent, jnp.float32)
    if pieces:
        drawn = drawn * block_levels(stream_key, extent, pieces, -0.22, 0.18)
    return jnp.clip(spiked(drawn, jax.random.fold_in(stream_key, 3), *heavy), -reach, reach).astype(dtype)


def setup_inputs(seed: int = 0) -> dict:
    keys = jax.random.split(jax.random.key(seed), 4)
    hidden_act = gaussian(keys[0], (TOKENS, FFW), 1.0, 6.0, ((0, 16), (1, 16)))
    out_grad = gaussian_with(keys[1], (TOKENS, D), 1.0, 6.0, ((0, 16), (1, 16)), (1, 0, 16, 2.0))
    down_weight = gaussian(keys[2], (FFW, D), D ** -0.5, 0.046875, ((0, 16), (1, 16)))
    return dict(hidden_act=hidden_act, out_grad=out_grad, down_weight=down_weight)


def reference(hidden_act, out_grad, down_weight):
    acts = hidden_act.reshape(EXAMPLES, SEQ, FFW)
    grads = out_grad.reshape(EXAMPLES, SEQ, D)

    def step(total, pair):
        grad_e = lax.dot_general(pair[0], pair[1], (((0,), (0,)), ((), ())), preferred_element_type=jnp.float32)
        return total + grad_e * grad_e, None

    total, unused = lax.scan(step, jnp.zeros((FFW, D), jnp.float32), (acts, grads))
    fisher = total / (EXAMPLES * SEQ)
    hidden_grad = lax.dot_general(out_grad, down_weight, (((1,), (1,)), ((), ())), preferred_element_type=jnp.float32)
    return fisher, hidden_grad.astype(jnp.bfloat16)
```

```python
import jax
import jax.numpy as jnp
from jax import lax
from jax.experimental import pallas as pl
from jax.experimental.pallas import tpu as pltpu
from jax.sharding import PartitionSpec as P

SEQ = 96
EXAMPLES = 8
MESH = pl.DeviceIdType.MESH

TOK = 48
HID = 1664
FEAT = 1024
TOKENS = 768

KINDS = []


def kind(name):
    if name not in KINDS:
        KINDS.append(name)
    return KINDS.index(name)


for j in range(3):
    kind(("gz", j))
for j in range(4):
    for name in ("gyp", "gym", "gyf"):
        kind((name, j))
for j in range(8):
    kind(("gc", j))
for name in ("az", "axp0", "axm0", "axp1", "axm1", "axf0", "axf1"):
    kind(name)
for j in range(8):
    kind(("ac", j))
kind("w")


def kernel(act, grad, weight, fisher, hidden, act_all, grad_all, grad_mate, w_all, left, part, recv,
           send_sems, recv_sems, part_send, part_recv, local_sems):
    r, c = lax.axis_index("row"), lax.axis_index("col")
    zh, y = r // 4, r % 4
    zl, x, core = c // 8, (c // 2) % 4, c % 2
    chip = c // 2

    def row_at(dzh, dy):
        return ((zh + dzh) % 4) * 4 + (y + dy) % 4

    def col_at(dzl, dx, dcore):
        return ((zl + dzl) % 2) * 8 + ((x + dx) % 4) * 2 + (core + dcore) % 2

    mate = (r, col_at(0, 0, 1))

    barrier = pltpu.get_barrier_semaphore()
    peers = [(row_at(dzh, 0), c) for dzh in (1, 2, 3)] + [(row_at(0, dy), c) for dy in (1, 3)]
    peers += [(r, col_at(dzl, dx, dc)) for dzl in range(2) for dx in range(4) for dc in range(2) if (dzl, dx, dc) != (0, 0, 0)]
    for peer in peers:
        pl.semaphore_signal(barrier, inc=1, device_id=peer, device_id_type=MESH)

    def rows(b):
        return pl.ds(pl.multiple_of(b * TOK, TOK), TOK)

    local = [
        pltpu.make_async_copy(grad, grad_all.at[rows(r)], local_sems.at[0]),
        pltpu.make_async_copy(act, act_all.at[rows(c)], local_sems.at[1]),
        pltpu.make_async_copy(weight, w_all.at[:, pl.ds(0, FEAT)], local_sems.at[2]),
    ]
    for copy in local:
        copy.start()
    pl.semaphore_wait(barrier, len(peers))

    sent = []

    def send(name, src, dst, to):
        k = kind(name)
        copy = pltpu.make_async_remote_copy(
            src_ref=src, dst_ref=dst, send_sem=send_sems.at[k], recv_sem=recv_sems.at[k],
            device_id=to, device_id_type=MESH,
        )
        copy.start()
        sent.append((name, copy))

    def arrived(name):
        for n, copy in sent:
            if n == name:
                copy.wait_recv()
                return
        raise ValueError(name)

    def send_grad(name, b, to, src=None):
        send(name, grad_all.at[rows(b)] if src is None else src, grad_all.at[rows(b)], to)

    def send_act(name, b, to, src=None):
        send(name, act_all.at[rows(b)] if src is None else src, act_all.at[rows(b)], to)

    zstep = (0, -1, 1, 2)

    def to_mate(first, y_block):
        for i in range(2):
            b = ((1 - core) + 2 * i) * 4 + y_block
            send(("gc", first + i), grad_all.at[rows(b)], grad_mate.at[rows(b)], mate)

    send_grad(("gz", 0), r, (row_at(1, 0), c), grad)
    send_grad(("gz", 1), r, (row_at(-1, 0), c), grad)
    send_grad(("gz", 2), r, (row_at(2, 0), c), grad)
    send_grad(("gyp", 0), r, (row_at(0, 1), c), grad)
    send_grad(("gym", 0), r, (row_at(0, -1), c), grad)
    send_act("az", c, (r, col_at(1, 0, 0)), act)
    send_act("axp0", c, (r, col_at(0, 1, 0)), act)
    send_act("axm0", c, (r, col_at(0, -1, 0)), act)
    send("w", weight, w_all.at[:, pl.ds(FEAT, FEAT)], mate)
    send_act(("ac", 0), c, mate, act)

    for j in (1, 2):
        arrived(("gz", j - 1))
        b = row_at(zstep[j], 0)
        send_grad(("gyp", j), b, (row_at(0, 1), c))
        send_grad(("gym", j), b, (row_at(0, -1), c))
    arrived("az")
    b = col_at(1, 0, 0)
    send_act("axp1", b, (r, col_at(0, 1, 0)))
    send_act("axm1", b, (r, col_at(0, -1, 0)))
    send_act(("ac", 1), b, mate)
    arrived(("gz", 2))
    b = row_at(2, 0)
    send_grad(("gyp", 3), b, (row_at(0, 1), c))
    send_grad(("gym", 3), b, (row_at(0, -1), c))
    for copy in local:
        copy.wait()
    to_mate(0, y)

    def forward_y(j):
        if j < 2:
            arrived(("gyp", j))
            send_grad(("gyf", j), row_at(zstep[j], -1), (row_at(0, 1), c))
        else:
            arrived(("gym", j))
            send_grad(("gyf", j), row_at(zstep[j], 1), (row_at(0, -1), c))

    forward_y(0)
    forward_y(1)
    forward_y(2)

    arrived("axp0")
    b = col_at(0, -1, 0)
    send_act("axf0", b, (r, col_at(0, 1, 0)))
    send_act(("ac", 2), b, mate)
    arrived("axm0")
    send_act(("ac", 3), col_at(0, 1, 0), mate)

    def multiply(first, y_blocks):
        blocks = [(core + 2 * i) * 4 + yb for yb in y_blocks for i in range(2)]
        count = len(blocks)
        for i, b in enumerate(blocks):
            left[pl.ds(i * TOK, TOK), pl.ds(0, FEAT)] = grad_all[rows(b), :]
            left[pl.ds(i * TOK, TOK), pl.ds(FEAT, FEAT)] = grad_mate[rows(b), :]

        def tile(start, width):
            value = lax.dot_general(
                left[pl.ds(0, count * TOK), :], w_all[pl.ds(start, width), :],
                (((1,), (1,)), ((), ())), preferred_element_type=jnp.float32,
            )
            for i in range(count):
                part[first + i, :, pl.ds(start, width)] = value[i * TOK:(i + 1) * TOK]

        @pl.loop(0, HID // 256)
        def _(n):
            tile(pl.multiple_of(n * 256, 256), 256)

        tile(HID // 256 * 256, HID % 256)
        for i, b in enumerate(blocks):
            @pl.when(b == c)
            def _():
                copy = pltpu.make_async_copy(part.at[first + i], recv.at[chip], part_recv.at[chip])
                copy.start()

            @pl.when(b != c)
            def _():
                pltpu.make_async_remote_copy(
                    src_ref=part.at[first + i], dst_ref=recv.at[chip], send_sem=part_send.at[first + i],
                    recv_sem=part_recv.at[chip], device_id=(r, b), device_id_type=MESH,
                ).start()
        return blocks

    arrived("w")
    arrived(("gc", 0))
    arrived(("gc", 1))
    dests = multiply(0, [y])

    forward_y(3)
    arrived("axm1")
    b = col_at(1, 1, 0)
    send_act("axf1", b, (r, col_at(0, -1, 0)))
    send_act(("ac", 4), b, mate)
    arrived("axp1")
    send_act(("ac", 5), col_at(1, -1, 0), mate)
    for j in (2, 3):
        arrived(("gyp", j))
    to_mate(2, (y - 1) % 4)
    for j in (0, 1):
        arrived(("gym", j))
    to_mate(4, (y + 1) % 4)
    for j in range(2, 6):
        arrived(("gc", j))
    dests += multiply(2, [(y - 1) % 4, (y + 1) % 4])

    for j in range(4):
        arrived(("gyf", j))
    to_mate(6, (y + 2) % 4)
    arrived("axf0")
    send_act(("ac", 6), col_at(0, 2, 0), mate)
    arrived("axf1")
    send_act(("ac", 7), col_at(1, 2, 0), mate)
    for j in range(6, 8):
        arrived(("gc", j))
    dests += multiply(6, [(y + 2) % 4])

    for j in range(8):
        arrived(("ac", j))

    @pl.loop(0, HID // 128)
    def _(n):
        start = pl.multiple_of(n * 128, 128)
        for f in range(FEAT // 256):
            total = jnp.zeros((128, 256), jnp.float32)
            for e in range(EXAMPLES):
                piece = lax.dot_general(
                    act_all[pl.ds(e * SEQ, SEQ), pl.ds(start, 128)], grad_all[pl.ds(e * SEQ, SEQ), pl.ds(f * 256, 256)],
                    (((0,), (0,)), ((), ())), preferred_element_type=jnp.float32,
                )
                total = total + piece * piece
            fisher[pl.ds(start, 128), pl.ds(f * 256, 256)] = total / (EXAMPLES * SEQ)

    for k in range(8):
        pltpu.make_async_copy(part.at[0], recv.at[k], part_recv.at[k]).wait()

    @pl.loop(0, TOK // 16)
    def _(n):
        at = pl.ds(pl.multiple_of(n * 16, 16), 16)
        total = recv[0, at, :]
        for k in range(1, 8):
            total = total + recv[k, at, :]
        hidden[at, :] = total.astype(jnp.bfloat16)

    for _, copy in sent:
        copy.wait_send()
    for i, b in enumerate(dests):
        @pl.when(b != c)
        def _():
            pltpu.make_async_remote_copy(
                src_ref=part.at[i], dst_ref=recv.at[chip], send_sem=part_send.at[i],
                recv_sem=part_recv.at[chip], device_id=(r, b), device_id_type=MESH,
            ).wait_send()


def per_device(hidden_act, out_grad, down_weight):
    any_spec = pl.BlockSpec(memory_space=pl.ANY)
    return pl.pallas_call(
        kernel,
        out_shape=(
            pltpu.VMEM((HID, FEAT), jnp.float32),
            jax.ShapeDtypeStruct((TOK, HID), jnp.bfloat16),
        ),
        in_specs=[any_spec] * 3,
        out_specs=(pl.BlockSpec(memory_space=pltpu.VMEM), pl.BlockSpec(memory_space=pltpu.VMEM)),
        scratch_shapes=[
            pltpu.VMEM((TOKENS, HID), jnp.bfloat16),
            pltpu.VMEM((TOKENS, FEAT), jnp.bfloat16),
            pltpu.VMEM((TOKENS, FEAT), jnp.bfloat16),
            pltpu.VMEM((HID, 2 * FEAT), jnp.bfloat16),
            pltpu.VMEM((4 * TOK, 2 * FEAT), jnp.bfloat16),
            pltpu.VMEM((8, TOK, HID), jnp.float32),
            pltpu.VMEM((8, TOK, HID), jnp.float32),
            pltpu.SemaphoreType.DMA((len(KINDS),)),
            pltpu.SemaphoreType.DMA((len(KINDS),)),
            pltpu.SemaphoreType.DMA((8,)),
            pltpu.SemaphoreType.DMA((8,)),
            pltpu.SemaphoreType.DMA((3,)),
        ],
        compiler_params=pltpu.CompilerParams(
            collective_id=0, has_side_effects=True, vmem_limit_bytes=36 * 1024 * 1024,
        ),
        name="fused_grads",
    )(hidden_act, out_grad, down_weight)


def solution(mesh):
    placed = (P("col", "row"), P("row", "col"), P("row", "col"))
    return jax.shard_map(
        per_device,
        mesh=mesh,
        in_specs=placed,
        out_specs=(P("row", "col"), P("col", "row")),
        check_vma=False,
    )
```

```python
import jax
import jax.numpy as jnp
from jax import lax
from jax.experimental import pallas as pl
from jax.experimental.pallas import tpu as pltpu
from jax.sharding import PartitionSpec as P

SEQ = 96
EXAMPLES = 8
MESH = pl.DeviceIdType.MESH

TOK = 48
HID = 1664
FEAT = 1024
TOKENS = 768
LANES = 128
SUB = 16
GROUPS = TOK // SUB
COLS = HID // LANES
TILES = GROUPS * COLS
RATE = 250.0
OFFSET = 125.0

KINDS = []


def kind(name):
    if name not in KINDS:
        KINDS.append(name)
    return KINDS.index(name)


for name in ("gz0", "gz1", "gz2", "gz3", "gy2"):
    kind(name)
for j in range(4):
    for name in ("gyp", "gym", "gyf"):
        kind((name, j))
for j in range(8):
    kind(("gc", j))
for name in ("az", "axp0", "axm0", "ax2", "axp1", "axm1", "axf1"):
    kind(name)
for j in range(8):
    kind(("ac", j))
kind("w")


def kernel(act, grad, weight, fisher, hidden, act_all, grad_all, grad_mate, w_all, w_t, left, raw, part, recv,
           send_sems, recv_sems, part_send, part_recv, local_sems):
    r, c = lax.axis_index("row"), lax.axis_index("col")
    zh, y = r // 4, r % 4
    zl, x, core = c // 8, (c // 2) % 4, c % 2
    chip = c // 2

    def row_at(dzh, dy):
        return ((zh + dzh) % 4) * 4 + (y + dy) % 4

    def col_at(dzl, dx, dcore):
        return ((zl + dzl) % 2) * 8 + ((x + dx) % 4) * 2 + (core + dcore) % 2

    mate = (r, col_at(0, 0, 1))

    barrier = pltpu.get_barrier_semaphore()
    peers = [(row_at(dzh, 0), c) for dzh in (1, 3)] + [(row_at(0, dy), c) for dy in (1, 2, 3)]
    peers += [(r, col_at(dzl, dx, dc)) for dzl in range(2) for dx in range(4) for dc in range(2) if (dzl, dx, dc) != (0, 0, 0)]
    for peer in peers:
        pl.semaphore_signal(barrier, inc=1, device_id=peer, device_id_type=MESH)

    def rows(b):
        return pl.ds(pl.multiple_of(b * TOK, TOK), TOK)

    local = [
        pltpu.make_async_copy(grad, grad_all.at[rows(r)], local_sems.at[0]),
        pltpu.make_async_copy(act, act_all.at[rows(c)], local_sems.at[1]),
        pltpu.make_async_copy(weight, w_all.at[0], local_sems.at[2]),
    ]
    for copy in local:
        copy.start()
    pl.semaphore_wait(barrier, len(peers))

    sent = []

    def send(name, src, dst, to):
        k = kind(name)
        copy = pltpu.make_async_remote_copy(
            src_ref=src, dst_ref=dst, send_sem=send_sems.at[k], recv_sem=recv_sems.at[k],
            device_id=to, device_id_type=MESH,
        )
        copy.start()
        sent.append((name, copy))

    def arrived(name):
        for n, copy in sent:
            if n == name:
                copy.wait_recv()
                return
        raise ValueError(name)

    def send_grad(name, b, to, src=None, columns=None):
        src, dst = grad_all.at[rows(b)] if src is None else src, grad_all.at[rows(b)]
        if columns is not None:
            src, dst = src.at[:, columns], dst.at[:, columns]
        send(name, src, dst, to)

    def send_act(name, b, to, src=None):
        send(name, act_all.at[rows(b)] if src is None else src, act_all.at[rows(b)], to)

    zstep = (0, -1, 1, 2)

    def to_mate(first, y_block):
        for i in range(2):
            b = ((1 - core) + 2 * i) * 4 + y_block
            send(("gc", first + i), grad_all.at[rows(b)], grad_mate.at[rows(b)], mate)

    def turn(half):
        @pl.loop(0, COLS)
        def _(n):
            at = pl.ds(pl.multiple_of(n * LANES, LANES), LANES)
            w_t[pl.ds(half * FEAT, FEAT), at] = w_all[half, at, :].T

    up, down, over = (row_at(0, 1), c), (row_at(0, -1), c), (row_at(0, 2), c)
    right, far = (r, col_at(0, 1, 0)), (r, col_at(0, 2, 0))
    back = (r, col_at(0, -1, 0))

    send_grad("gz0", r, (row_at(1, 0), c), grad)
    send_grad("gz1", r, (row_at(-1, 0), c), grad)
    send_grad(("gyp", 0), r, up, grad)
    send_grad(("gym", 0), r, down, grad)
    send_grad("gy2", r, over, grad)
    send_act("axp0", c, right, act)
    send_act("axm0", c, back, act)
    send("w", weight, w_all.at[1], mate)
    send_act("ax2", c, far, act)
    send_act(("ac", 0), c, mate, act)
    local[2].wait()
    turn(0)

    half = FEAT // 2
    arrived("gz0")
    send_grad("gz2", row_at(-1, 0), (row_at(1, 0), c), columns=pl.ds(0, half))
    arrived("gz1")
    send_grad("gz3", row_at(1, 0), (row_at(-1, 0), c), columns=pl.ds(half, half))
    for j in (1, 2):
        send_grad(("gyp", j), row_at(zstep[j], 0), up)
        send_grad(("gym", j), row_at(zstep[j], 0), down)
    send_act("az", c, (r, col_at(1, 0, 0)), act)
    local[0].wait()
    local[1].wait()
    arrived("gz2")
    arrived("gz3")
    send_grad(("gyp", 3), row_at(2, 0), up)
    send_grad(("gym", 3), row_at(2, 0), down)
    to_mate(0, y)
    arrived("az")
    b = col_at(1, 0, 0)
    send_act("axp1", b, right)
    send_act("axm1", b, back)
    send_act(("ac", 1), b, mate)

    def forward_y(j):
        if j < 2:
            arrived(("gyp", j))
            send_grad(("gyf", j), row_at(zstep[j], -1), up)
        else:
            arrived(("gym", j))
            send_grad(("gyf", j), row_at(zstep[j], 1), down)

    forward_y(1)
    forward_y(2)
    arrived("axp0")
    send_act(("ac", 2), col_at(0, -1, 0), mate)
    arrived("axm0")
    send_act(("ac", 3), col_at(0, 1, 0), mate)
    forward_y(3)
    arrived("ax2")
    send_act(("ac", 6), col_at(0, 2, 0), mate)
    arrived("axm1")
    b = col_at(1, 1, 0)
    send_act("axf1", b, back)
    send_act(("ac", 4), b, mate)
    arrived("w")
    turn(1)

    def multiply(first, y_blocks):
        blocks = [(core + 2 * i) * 4 + yb for yb in y_blocks for i in range(2)]
        count = len(blocks)
        for i, b in enumerate(blocks):
            left[pl.ds(i * TOK, TOK), pl.ds(0, FEAT)] = grad_all[rows(b), :]
            left[pl.ds(i * TOK, TOK), pl.ds(FEAT, FEAT)] = grad_mate[rows(b), :]

        raw[pl.ds(0, count * TOK), :] = jnp.dot(
            left[pl.ds(0, count * TOK), :], w_t[...], preferred_element_type=jnp.float32
        )

        @pl.loop(0, count)
        def _(i):
            lane = lax.broadcasted_iota(jnp.int32, (SUB, LANES), 1)
            scales = jnp.zeros((SUB, LANES), jnp.float32)
            for g in range(GROUPS):
                at = pl.ds(pl.multiple_of(i * TOK + g * SUB, SUB), SUB)
                top = jnp.max(jnp.abs(raw[at, :]), axis=1, keepdims=True)
                top = top.astype(jnp.bfloat16).astype(jnp.float32)
                inverse = jnp.where(top > 0, 1.0 / jnp.where(top > 0, top, 1.0), 0.0)
                scales = jnp.where(lane // 32 == g, top, scales)
                for n in range(COLS):
                    value = raw[at, pl.ds(n * LANES, LANES)]
                    level = jnp.abs(value) * inverse + 1e-30
                    code = jnp.exp2(RATE * level * lax.rsqrt(level) - OFFSET)
                    part[first + i, g * COLS + n] = jnp.where(value < 0, -code, code).astype(jnp.bfloat16)
            part[first + i, TILES] = scales.astype(jnp.bfloat16)

            yb = y_blocks[0] if len(y_blocks) == 1 else jnp.where(i < 2, y_blocks[0], y_blocks[1])
            b = (core + 2 * (i % 2)) * 4 + yb

            @pl.when(b == c)
            def _():
                pltpu.make_async_copy(part.at[first + i], recv.at[chip], part_recv.at[chip]).start()

            @pl.when(b != c)
            def _():
                pltpu.make_async_remote_copy(
                    src_ref=part.at[first + i], dst_ref=recv.at[chip], send_sem=part_send.at[first + i],
                    recv_sem=part_recv.at[chip], device_id=(r, b), device_id_type=MESH,
                ).start()

        return blocks

    arrived(("gc", 0))
    arrived(("gc", 1))
    dests = multiply(0, [y])

    arrived("axp1")
    send_act(("ac", 5), col_at(1, -1, 0), mate)
    for j in (0, 2, 3):
        arrived(("gyp", j))
    to_mate(2, (y - 1) % 4)
    for j in (0, 1):
        arrived(("gym", j))
    to_mate(4, (y + 1) % 4)
    arrived("axf1")
    send_act(("ac", 7), col_at(1, 2, 0), mate)
    for j in range(2, 6):
        arrived(("gc", j))
    dests += multiply(2, [(y - 1) % 4, (y + 1) % 4])

    arrived("gy2")
    for j in range(1, 4):
        arrived(("gyf", j))
    to_mate(6, (y + 2) % 4)
    for j in range(6, 8):
        arrived(("gc", j))
    dests += multiply(6, [(y + 2) % 4])

    for j in range(8):
        arrived(("ac", j))

    def fisher_rows(start, height):
        for f in range(FEAT // 256):
            total = None
            for e in range(EXAMPLES):
                piece = lax.dot_general(
                    act_all[pl.ds(e * SEQ, SEQ), pl.ds(start, height)], grad_all[pl.ds(e * SEQ, SEQ), pl.ds(f * 256, 256)],
                    (((0,), (0,)), ((), ())), preferred_element_type=jnp.float32,
                )
                total = piece * piece if total is None else total + piece * piece
            fisher[pl.ds(start, height), pl.ds(f * 256, 256)] = total * (1.0 / (EXAMPLES * SEQ))

    @pl.loop(0, HID // 512)
    def _(n):
        fisher_rows(pl.multiple_of(n * 512, 512), 512)

    fisher_rows(HID // 512 * 512, HID % 512)

    for k in range(8):
        pltpu.make_async_copy(part.at[0], recv.at[k], part_recv.at[k]).wait()

    for g in range(GROUPS):
        scales = [recv[k, TILES, :, pl.ds(g * 32, 1)].astype(jnp.float32) * (1.0 / RATE ** 2) for k in range(8)]

        for n in range(COLS):
            total = jnp.zeros((SUB, LANES), jnp.float32)
            for k in range(8):
                code = recv[k, g * COLS + n].astype(jnp.float32)
                level = jnp.log2(jnp.abs(code)) + OFFSET
                value = scales[k] * level * level
                total = total + jnp.where(code < 0, -value, value)
            hidden[pl.ds(g * SUB, SUB), pl.ds(n * LANES, LANES)] = total.astype(jnp.bfloat16)

    for _, copy in sent:
        copy.wait_send()
    for i, b in enumerate(dests):
        @pl.when(b != c)
        def _():
            pltpu.make_async_remote_copy(
                src_ref=part.at[i], dst_ref=recv.at[chip], send_sem=part_send.at[i],
                recv_sem=part_recv.at[chip], device_id=(r, b), device_id_type=MESH,
            ).wait_send()


def per_device(hidden_act, out_grad, down_weight):
    any_spec = pl.BlockSpec(memory_space=pl.ANY)
    return pl.pallas_call(
        kernel,
        out_shape=(
            pltpu.VMEM((HID, FEAT), jnp.float32),
            jax.ShapeDtypeStruct((TOK, HID), jnp.bfloat16),
        ),
        in_specs=[any_spec] * 3,
        out_specs=(pl.BlockSpec(memory_space=pltpu.VMEM), pl.BlockSpec(memory_space=pltpu.VMEM)),
        scratch_shapes=[
            pltpu.VMEM((TOKENS, HID), jnp.bfloat16),
            pltpu.VMEM((TOKENS, FEAT), jnp.bfloat16),
            pltpu.VMEM((TOKENS, FEAT), jnp.bfloat16),
            pltpu.VMEM((2, HID, FEAT), jnp.bfloat16),
            pltpu.VMEM((2 * FEAT, HID), jnp.bfloat16),
            pltpu.VMEM((4 * TOK, 2 * FEAT), jnp.bfloat16),
            pltpu.VMEM((4 * TOK, HID), jnp.float32),
            pltpu.VMEM((8, TILES + 1, SUB, LANES), jnp.bfloat16),
            pltpu.VMEM((8, TILES + 1, SUB, LANES), jnp.bfloat16),
            pltpu.SemaphoreType.DMA((len(KINDS),)),
            pltpu.SemaphoreType.DMA((len(KINDS),)),
            pltpu.SemaphoreType.DMA((8,)),
            pltpu.SemaphoreType.DMA((8,)),
            pltpu.SemaphoreType.DMA((3,)),
        ],
        compiler_params=pltpu.CompilerParams(
            collective_id=0, has_side_effects=True, vmem_limit_bytes=60 * 1000 * 1000,
        ),
        name="fused_grads",
    )(hidden_act, out_grad, down_weight)


def solution(mesh):
    placed = (P("col", "row"), P("row", "col"), P("row", "col"))
    return jax.shard_map(
        per_device,
        mesh=mesh,
        in_specs=placed,
        out_specs=(P("row", "col"), P("col", "row")),
        check_vma=False,
    )
```

```python
import jax
import jax.numpy as jnp
from jax import lax
from jax.experimental import pallas as pl
from jax.experimental.pallas import tpu as pltpu
from jax.sharding import PartitionSpec as P

SEQ = 96
EXAMPLES = 8
MESH = pl.DeviceIdType.MESH

TOK = 48
HID = 1664
FEAT = 1024
TOKENS = 768
LANES = 128
SUB = 16
GROUPS = TOK // SUB
COLS = HID // LANES
TILES = GROUPS * COLS
CHUNKS = 8
RATE = 250.0
OFFSET = 125.0

KINDS = []


def kind(name):
    if name not in KINDS:
        KINDS.append(name)
    return KINDS.index(name)


for name in ("gz0", "gz1", "gz2", "gz3", "gy2"):
    kind(name)
for j in range(4):
    for name in ("gyp", "gym", "gyf"):
        kind((name, j))
for j in range(8):
    kind(("gc", j))
for name in ("az", "axp0", "axm0", "ax2", "axp1", "axm1", "axf1"):
    kind(name)
for j in range(8):
    kind(("ac", j))
kind("w")


def kernel(act, grad, weight, fisher, recv, act_all, grad_all, grad_mate, w_all, w_t, left, raw, part,
           send_sems, recv_sems, part_send, part_recv, local_sems):
    r, c = lax.axis_index("row"), lax.axis_index("col")
    zh, y = r // 4, r % 4
    zl, x, core = c // 8, (c // 2) % 4, c % 2
    chip = c // 2

    def row_at(dzh, dy):
        return ((zh + dzh) % 4) * 4 + (y + dy) % 4

    def col_at(dzl, dx, dcore):
        return ((zl + dzl) % 2) * 8 + ((x + dx) % 4) * 2 + (core + dcore) % 2

    mate = (r, col_at(0, 0, 1))

    barrier = pltpu.get_barrier_semaphore()
    peers = [(row_at(dzh, 0), c) for dzh in (1, 3)] + [(row_at(0, dy), c) for dy in (1, 2, 3)]
    peers += [(r, col_at(dzl, dx, dc)) for dzl in range(2) for dx in range(4) for dc in range(2) if (dzl, dx, dc) != (0, 0, 0)]
    for peer in peers:
        pl.semaphore_signal(barrier, inc=1, device_id=peer, device_id_type=MESH)

    def rows(b):
        return pl.ds(pl.multiple_of(b * TOK, TOK), TOK)

    local = [
        pltpu.make_async_copy(grad, grad_all.at[rows(r)], local_sems.at[0]),
        pltpu.make_async_copy(act, act_all.at[rows(c)], local_sems.at[1]),
        pltpu.make_async_copy(weight, w_all.at[0], local_sems.at[2]),
    ]
    for copy in local:
        copy.start()
    pl.semaphore_wait(barrier, len(peers))

    sent = []

    def send(name, src, dst, to):
        k = kind(name)
        copy = pltpu.make_async_remote_copy(
            src_ref=src, dst_ref=dst, send_sem=send_sems.at[k], recv_sem=recv_sems.at[k],
            device_id=to, device_id_type=MESH,
        )
        copy.start()
        sent.append((name, copy))

    def arrived(name):
        for n, copy in sent:
            if n == name:
                copy.wait_recv()
                return
        raise ValueError(name)

    def send_grad(name, b, to, src=None, columns=None):
        src, dst = grad_all.at[rows(b)] if src is None else src, grad_all.at[rows(b)]
        if columns is not None:
            src, dst = src.at[:, columns], dst.at[:, columns]
        send(name, src, dst, to)

    def send_act(name, b, to, src=None):
        send(name, act_all.at[rows(b)] if src is None else src, act_all.at[rows(b)], to)

    zstep = (0, -1, 1, 2)

    def to_mate(first, y_block):
        for i in range(2):
            b = ((1 - core) + 2 * i) * 4 + y_block
            send(("gc", first + i), grad_all.at[rows(b)], grad_mate.at[rows(b)], mate)

    def turn(half):
        @pl.loop(0, COLS)
        def _(n):
            at = pl.ds(pl.multiple_of(n * LANES, LANES), LANES)
            w_t[pl.ds(half * FEAT, FEAT), at] = w_all[half, at, :].T

    up, down, over = (row_at(0, 1), c), (row_at(0, -1), c), (row_at(0, 2), c)
    right, far = (r, col_at(0, 1, 0)), (r, col_at(0, 2, 0))
    back = (r, col_at(0, -1, 0))

    def multiply(first, y_blocks):
        blocks = [(core + 2 * i) * 4 + yb for yb in y_blocks for i in range(2)]
        count = len(blocks)
        for i, b in enumerate(blocks):
            left[pl.ds(i * TOK, TOK), pl.ds(0, FEAT)] = grad_all[rows(b), :]
            left[pl.ds(i * TOK, TOK), pl.ds(FEAT, FEAT)] = grad_mate[rows(b), :]

        raw[pl.ds(0, count * TOK), :] = jnp.dot(
            left[pl.ds(0, count * TOK), :], w_t[...], preferred_element_type=jnp.float32
        )

        @pl.loop(0, count)
        def _(i):
            lane = lax.broadcasted_iota(jnp.int32, (SUB, LANES), 1)
            scales = jnp.zeros((SUB, LANES), jnp.float32)
            for g in range(GROUPS):
                at = pl.ds(pl.multiple_of(i * TOK + g * SUB, SUB), SUB)
                top = jnp.max(jnp.abs(raw[at, :]), axis=1, keepdims=True)
                top = top.astype(jnp.bfloat16).astype(jnp.float32)
                inverse = jnp.where(top > 0, 1.0 / jnp.where(top > 0, top, 1.0), 0.0)
                scales = jnp.where(lane // 32 == g, top, scales)
                for n in range(COLS):
                    value = raw[at, pl.ds(n * LANES, LANES)]
                    level = jnp.abs(value) * inverse + 1e-30
                    code = jnp.exp2(RATE * level * lax.rsqrt(level) - OFFSET)
                    part[first + i, g * COLS + n] = jnp.where(value < 0, -code, code).astype(jnp.bfloat16)
            part[first + i, TILES] = scales.astype(jnp.bfloat16)

            yb = y_blocks[0] if len(y_blocks) == 1 else jnp.where(i < 2, y_blocks[0], y_blocks[1])
            b = (core + 2 * (i % 2)) * 4 + yb

            @pl.when(b == c)
            def _():
                pltpu.make_async_copy(part.at[first + i], recv.at[chip], part_recv.at[chip]).start()

            @pl.when(b != c)
            def _():
                pltpu.make_async_remote_copy(
                    src_ref=part.at[first + i], dst_ref=recv.at[chip], send_sem=part_send.at[first + i],
                    recv_sem=part_recv.at[chip], device_id=(r, b), device_id_type=MESH,
                ).start()

        return blocks

    send_grad("gz0", r, (row_at(1, 0), c), grad)
    send_grad("gz1", r, (row_at(-1, 0), c), grad)
    send_grad(("gyp", 0), r, up, grad)
    send_grad(("gym", 0), r, down, grad)
    send_grad("gy2", r, over, grad)
    send_act("axp0", c, right, act)
    send_act("axm0", c, back, act)
    send("w", weight, w_all.at[1], mate)
    send_act("ax2", c, far, act)
    send_act(("ac", 0), c, mate, act)
    local[2].wait()
    turn(0)

    half = FEAT // 2
    arrived("gz0")
    send_grad("gz2", row_at(-1, 0), (row_at(1, 0), c), columns=pl.ds(0, half))
    arrived("gz1")
    send_grad("gz3", row_at(1, 0), (row_at(-1, 0), c), columns=pl.ds(half, half))
    for j in (1, 2):
        send_grad(("gyp", j), row_at(zstep[j], 0), up)
        send_grad(("gym", j), row_at(zstep[j], 0), down)
    send_act("az", c, (r, col_at(1, 0, 0)), act)
    local[0].wait()
    local[1].wait()
    arrived("gz2")
    arrived("gz3")
    send_grad(("gyp", 3), row_at(2, 0), up)
    send_grad(("gym", 3), row_at(2, 0), down)
    to_mate(0, y)
    arrived("az")
    b = col_at(1, 0, 0)
    send_act("axp1", b, right)
    send_act("axm1", b, back)
    send_act(("ac", 1), b, mate)

    def forward_y(j):
        if j < 2:
            arrived(("gyp", j))
            send_grad(("gyf", j), row_at(zstep[j], -1), up)
        else:
            arrived(("gym", j))
            send_grad(("gyf", j), row_at(zstep[j], 1), down)

    forward_y(1)
    forward_y(2)
    arrived("w")
    turn(1)
    arrived(("gc", 0))
    arrived(("gc", 1))
    dests = multiply(0, [y])

    forward_y(3)
    for j in (0, 2, 3):
        arrived(("gyp", j))
    to_mate(2, (y - 1) % 4)
    for j in (0, 1):
        arrived(("gym", j))
    to_mate(4, (y + 1) % 4)
    arrived("axp0")
    send_act(("ac", 2), col_at(0, -1, 0), mate)
    arrived("axm0")
    send_act(("ac", 3), col_at(0, 1, 0), mate)
    arrived("ax2")
    send_act(("ac", 6), col_at(0, 2, 0), mate)
    arrived("axm1")
    b = col_at(1, 1, 0)
    send_act("axf1", b, back)
    send_act(("ac", 4), b, mate)
    for j in range(2, 6):
        arrived(("gc", j))
    dests += multiply(2, [(y - 1) % 4, (y + 1) % 4])

    arrived("axp1")
    send_act(("ac", 5), col_at(1, -1, 0), mate)
    arrived("axf1")
    send_act(("ac", 7), col_at(1, 2, 0), mate)
    arrived("gy2")
    for j in range(1, 4):
        arrived(("gyf", j))
    to_mate(6, (y + 2) % 4)
    for j in range(6, 8):
        arrived(("gc", j))
    dests += multiply(6, [(y + 2) % 4])

    for j in range(8):
        arrived(("ac", j))

    def fisher_rows(start, height):
        for f in range(FEAT // 256):
            total = None
            for e in range(EXAMPLES):
                piece = lax.dot_general(
                    act_all[pl.ds(e * SEQ, SEQ), pl.ds(start, height)], grad_all[pl.ds(e * SEQ, SEQ), pl.ds(f * 256, 256)],
                    (((0,), (0,)), ((), ())), preferred_element_type=jnp.float32,
                )
                total = piece * piece if total is None else total + piece * piece
            fisher[pl.ds(start, height), pl.ds(f * 256, 256)] = total * (1.0 / (EXAMPLES * SEQ))

    @pl.loop(0, HID // 512)
    def _(n):
        fisher_rows(pl.multiple_of(n * 512, 512), 512)

    fisher_rows(HID // 512 * 512, HID % 512)

    for k in range(8):
        pltpu.make_async_copy(part.at[0], recv.at[k], part_recv.at[k]).wait()

    for _, copy in sent:
        copy.wait_send()
    for i, b in enumerate(dests):
        @pl.when(b != c)
        def _():
            pltpu.make_async_remote_copy(
                src_ref=part.at[i], dst_ref=recv.at[chip], send_sem=part_send.at[i],
                recv_sem=part_recv.at[chip], device_id=(r, b), device_id_type=MESH,
            ).wait_send()


def finish(fisher, recv, fisher_out, hidden_out, hidden, sems):
    height = HID // CHUNKS
    copies = [
        pltpu.make_async_copy(fisher.at[pl.ds(i * height, height)], fisher_out.at[pl.ds(i * height, height)], sems.at[i])
        for i in range(CHUNKS)
    ]
    for copy in copies:
        copy.start()
    for g in range(GROUPS):
        scales = [recv[k, TILES, :, pl.ds(g * 32, 1)].astype(jnp.float32) * (1.0 / RATE ** 2) for k in range(8)]

        for n in range(COLS):
            total = jnp.zeros((SUB, LANES), jnp.float32)
            for k in range(8):
                code = recv[k, g * COLS + n].astype(jnp.float32)
                level = jnp.log2(jnp.abs(code)) + OFFSET
                value = scales[k] * level * level
                total = total + jnp.where(code < 0, -value, value)
            hidden[pl.ds(g * SUB, SUB), pl.ds(n * LANES, LANES)] = total.astype(jnp.bfloat16)

    last = pltpu.make_async_copy(hidden, hidden_out, sems.at[CHUNKS])
    last.start()
    for copy in copies:
        copy.wait()
    last.wait()


def per_device(hidden_act, out_grad, down_weight):
    any_spec = pl.BlockSpec(memory_space=pl.ANY)
    fisher, recv = pl.pallas_call(
        kernel,
        out_shape=(
            pltpu.VMEM((HID, FEAT), jnp.float32),
            pltpu.VMEM((8, TILES + 1, SUB, LANES), jnp.bfloat16),
        ),
        in_specs=[any_spec] * 3,
        out_specs=(pl.BlockSpec(memory_space=pltpu.VMEM), pl.BlockSpec(memory_space=pltpu.VMEM)),
        scratch_shapes=[
            pltpu.VMEM((TOKENS, HID), jnp.bfloat16),
            pltpu.VMEM((TOKENS, FEAT), jnp.bfloat16),
            pltpu.VMEM((TOKENS, FEAT), jnp.bfloat16),
            pltpu.VMEM((2, HID, FEAT), jnp.bfloat16),
            pltpu.VMEM((2 * FEAT, HID), jnp.bfloat16),
            pltpu.VMEM((4 * TOK, 2 * FEAT), jnp.bfloat16),
            pltpu.VMEM((4 * TOK, HID), jnp.float32),
            pltpu.VMEM((8, TILES + 1, SUB, LANES), jnp.bfloat16),
            pltpu.SemaphoreType.DMA((len(KINDS),)),
            pltpu.SemaphoreType.DMA((len(KINDS),)),
            pltpu.SemaphoreType.DMA((8,)),
            pltpu.SemaphoreType.DMA((8,)),
            pltpu.SemaphoreType.DMA((3,)),
        ],
        compiler_params=pltpu.CompilerParams(
            collective_id=0, has_side_effects=True, vmem_limit_bytes=58300 * 1000,
        ),
        name="fused_grads",
    )(hidden_act, out_grad, down_weight)
    return pl.pallas_call(
        finish,
        out_shape=(
            jax.ShapeDtypeStruct((HID, FEAT), jnp.float32),
            jax.ShapeDtypeStruct((TOK, HID), jnp.bfloat16),
        ),
        in_specs=[any_spec, pl.BlockSpec(memory_space=pltpu.VMEM)],
        out_specs=(any_spec, any_spec),
        scratch_shapes=[pltpu.VMEM((TOK, HID), jnp.bfloat16), pltpu.SemaphoreType.DMA((CHUNKS + 1,))],
        compiler_params=pltpu.CompilerParams(vmem_limit_bytes=40 * 1000 * 1000),
        name="write_out",
    )(fisher, recv)


def solution(mesh):
    placed = (P("col", "row"), P("row", "col"), P("row", "col"))
    return jax.shard_map(
        per_device,
        mesh=mesh,
        in_specs=placed,
        out_specs=(P("row", "col"), P("col", "row")),
        check_vma=False,
    )
```

```python
import jax
import jax.numpy as jnp
from jax import lax
from jax.experimental import pallas as pl
from jax.experimental.pallas import tpu as pltpu
from jax.sharding import PartitionSpec as P

SEQ = 96
EXAMPLES = 8
MESH = pl.DeviceIdType.MESH

TOK = 48
HID = 1664
FEAT = 1024
TOKENS = 768
LANES = 128
SUB = 16
GROUPS = TOK // SUB
COLS = HID // LANES
TILES = GROUPS * COLS
CHUNKS = 8
RATE = 250.0
OFFSET = 125.0

KINDS = []


def kind(name):
    if name not in KINDS:
        KINDS.append(name)
    return KINDS.index(name)


for name in ("gz0", "gz1", "gz2", "gz3", "gy2"):
    kind(name)
for j in range(4):
    for name in ("gyp", "gym", "gyf"):
        kind((name, j))
for j in range(8):
    kind(("gc", j))
for name in ("az", "axp0", "axm0", "ax2", "axp1", "axm1", "axf1"):
    kind(name)
for j in range(8):
    kind(("ac", j))
kind("w")


def kernel(act, grad, weight, fisher, recv, act_all, grad_all, grad_mate, w_all, w_t, left, raw, part,
           send_sems, recv_sems, part_send, part_recv, local_sems):
    r, c = lax.axis_index("row"), lax.axis_index("col")
    zh, y = r // 4, r % 4
    zl, x, core = c // 8, (c // 2) % 4, c % 2
    chip = c // 2

    def row_at(dzh, dy):
        return ((zh + dzh) % 4) * 4 + (y + dy) % 4

    def col_at(dzl, dx, dcore):
        return ((zl + dzl) % 2) * 8 + ((x + dx) % 4) * 2 + (core + dcore) % 2

    mate = (r, col_at(0, 0, 1))

    barrier = pltpu.get_barrier_semaphore()
    peers = [(row_at(dzh, 0), c) for dzh in (1, 3)] + [(row_at(0, dy), c) for dy in (1, 2, 3)]
    peers += [(r, col_at(dzl, dx, dc)) for dzl in range(2) for dx in range(4) for dc in range(2) if (dzl, dx, dc) != (0, 0, 0)]
    for peer in peers:
        pl.semaphore_signal(barrier, inc=1, device_id=peer, device_id_type=MESH)

    def rows(b):
        return pl.ds(pl.multiple_of(b * TOK, TOK), TOK)

    local = [
        pltpu.make_async_copy(grad, grad_all.at[rows(r)], local_sems.at[0]),
        pltpu.make_async_copy(act, act_all.at[rows(c)], local_sems.at[1]),
        pltpu.make_async_copy(weight, w_all.at[0], local_sems.at[2]),
    ]
    for copy in local:
        copy.start()
    pl.semaphore_wait(barrier, len(peers))

    sent = []

    def send(name, src, dst, to):
        k = kind(name)
        copy = pltpu.make_async_remote_copy(
            src_ref=src, dst_ref=dst, send_sem=send_sems.at[k], recv_sem=recv_sems.at[k],
            device_id=to, device_id_type=MESH,
        )
        copy.start()
        sent.append((name, copy))

    def arrived(name):
        for n, copy in sent:
            if n == name:
                copy.wait_recv()
                return
        raise ValueError(name)

    def send_grad(name, b, to, src=None, columns=None):
        src, dst = grad_all.at[rows(b)] if src is None else src, grad_all.at[rows(b)]
        if columns is not None:
            src, dst = src.at[:, columns], dst.at[:, columns]
        send(name, src, dst, to)

    def send_act(name, b, to, src=None):
        send(name, act_all.at[rows(b)] if src is None else src, act_all.at[rows(b)], to)

    zstep = (0, -1, 1, 2)

    def to_mate(first, y_block):
        for i in range(2):
            b = ((1 - core) + 2 * i) * 4 + y_block
            send(("gc", first + i), grad_all.at[rows(b)], grad_mate.at[rows(b)], mate)

    def turn(half):
        @pl.loop(0, COLS)
        def _(n):
            at = pl.ds(pl.multiple_of(n * LANES, LANES), LANES)
            w_t[pl.ds(half * FEAT, FEAT), at] = w_all[half, at, :].T

    up, down, over = (row_at(0, 1), c), (row_at(0, -1), c), (row_at(0, 2), c)
    right, far = (r, col_at(0, 1, 0)), (r, col_at(0, 2, 0))
    back = (r, col_at(0, -1, 0))

    def multiply(first, y_blocks):
        blocks = [(core + 2 * i) * 4 + yb for yb in y_blocks for i in range(2)]
        count = len(blocks)
        for i, b in enumerate(blocks):
            left[pl.ds(i * TOK, TOK), pl.ds(0, FEAT)] = grad_all[rows(b), :]
            left[pl.ds(i * TOK, TOK), pl.ds(FEAT, FEAT)] = grad_mate[rows(b), :]

        raw[pl.ds(0, count * TOK), :] = jnp.dot(
            left[pl.ds(0, count * TOK), :], w_t[...], preferred_element_type=jnp.float32
        )

        @pl.loop(0, count)
        def _(i):
            lane = lax.broadcasted_iota(jnp.int32, (SUB, LANES), 1)
            scales = jnp.zeros((SUB, LANES), jnp.float32)
            for g in range(GROUPS):
                at = pl.ds(pl.multiple_of(i * TOK + g * SUB, SUB), SUB)
                top = jnp.max(jnp.abs(raw[at, :]), axis=1, keepdims=True)
                top = top.astype(jnp.bfloat16).astype(jnp.float32)
                inverse = jnp.where(top > 0, 1.0 / jnp.where(top > 0, top, 1.0), 0.0)
                scales = jnp.where(lane // 32 == g, top, scales)
                for n in range(COLS):
                    value = raw[at, pl.ds(n * LANES, LANES)]
                    level = jnp.abs(value) * inverse + 1e-30
                    code = jnp.exp2(RATE * level * lax.rsqrt(level) - OFFSET)
                    part[first + i, g * COLS + n] = jnp.where(value < 0, -code, code).astype(jnp.bfloat16)
            part[first + i, TILES] = scales.astype(jnp.bfloat16)

            yb = y_blocks[0] if len(y_blocks) == 1 else jnp.where(i < 2, y_blocks[0], y_blocks[1])
            b = (core + 2 * (i % 2)) * 4 + yb

            @pl.when(b == c)
            def _():
                pltpu.make_async_copy(part.at[first + i], recv.at[chip], part_recv.at[chip]).start()

            @pl.when(b != c)
            def _():
                pltpu.make_async_remote_copy(
                    src_ref=part.at[first + i], dst_ref=recv.at[chip], send_sem=part_send.at[first + i],
                    recv_sem=part_recv.at[chip], device_id=(r, b), device_id_type=MESH,
                ).start()

        return blocks

    send_grad("gz0", r, (row_at(1, 0), c), grad)
    send_grad("gz1", r, (row_at(-1, 0), c), grad)
    send_grad(("gyp", 0), r, up, grad)
    send_grad(("gym", 0), r, down, grad)
    send_grad("gy2", r, over, grad)
    send_act("axp0", c, right, act)
    send_act("axm0", c, back, act)
    send("w", weight, w_all.at[1], mate)
    send_act("ax2", c, far, act)
    send_act(("ac", 0), c, mate, act)
    local[2].wait()
    turn(0)

    half = FEAT // 2
    arrived("gz0")
    send_grad("gz2", row_at(-1, 0), (row_at(1, 0), c), columns=pl.ds(0, half))
    arrived("gz1")
    send_grad("gz3", row_at(1, 0), (row_at(-1, 0), c), columns=pl.ds(half, half))
    for j in (1, 2):
        send_grad(("gyp", j), row_at(zstep[j], 0), up)
        send_grad(("gym", j), row_at(zstep[j], 0), down)
    send_act("az", c, (r, col_at(1, 0, 0)), act)
    local[0].wait()
    local[1].wait()
    arrived("gz2")
    arrived("gz3")
    send_grad(("gyp", 3), row_at(2, 0), up)
    send_grad(("gym", 3), row_at(2, 0), down)
    to_mate(0, y)
    arrived("az")
    b = col_at(1, 0, 0)
    send_act("axp1", b, right)
    send_act("axm1", b, back)
    send_act(("ac", 1), b, mate)

    def forward_y(j):
        if j < 2:
            arrived(("gyp", j))
            send_grad(("gyf", j), row_at(zstep[j], -1), up)
        else:
            arrived(("gym", j))
            send_grad(("gyf", j), row_at(zstep[j], 1), down)

    forward_y(1)
    forward_y(2)
    arrived("w")
    turn(1)
    arrived(("gc", 0))
    arrived(("gc", 1))
    dests = multiply(0, [y])

    forward_y(3)
    for j in (0, 2, 3):
        arrived(("gyp", j))
    to_mate(2, (y - 1) % 4)
    for j in (0, 1):
        arrived(("gym", j))
    to_mate(4, (y + 1) % 4)
    arrived("axp0")
    send_act(("ac", 2), col_at(0, -1, 0), mate)
    arrived("axm0")
    send_act(("ac", 3), col_at(0, 1, 0), mate)
    arrived("ax2")
    send_act(("ac", 6), col_at(0, 2, 0), mate)
    for j in range(2, 6):
        arrived(("gc", j))
    dests += multiply(2, [(y - 1) % 4, (y + 1) % 4])

    arrived("axm1")
    b = col_at(1, 1, 0)
    send_act("axf1", b, back)
    send_act(("ac", 4), b, mate)
    arrived("gy2")
    for j in range(1, 4):
        arrived(("gyf", j))
    to_mate(6, (y + 2) % 4)
    for j in range(6, 8):
        arrived(("gc", j))
    dests += multiply(6, [(y + 2) % 4])

    early = [zl * 4 + e for e in range(4)] + [col_at(1, 0, 0) // 2, col_at(1, 1, 0) // 2]
    late = [col_at(1, 2, 0) // 2, col_at(1, 3, 0) // 2]

    def fisher_rows(start, height, examples, is_last):
        for f in range(FEAT // 256):
            at = pl.ds(start, height), pl.ds(f * 256, 256)
            total = fisher[at] if is_last else None
            for e in examples:
                tokens = pl.ds(pl.multiple_of(e * SEQ, SEQ), SEQ)
                piece = lax.dot_general(
                    act_all[tokens, pl.ds(start, height)], grad_all[tokens, pl.ds(f * 256, 256)],
                    (((0,), (0,)), ((), ())), preferred_element_type=jnp.float32,
                )
                total = piece * piece if total is None else total + piece * piece
            fisher[at] = total * (1.0 / (EXAMPLES * SEQ)) if is_last else total

    for j in (0, 1, 2, 3, 4, 6):
        arrived(("ac", j))

    fisher_rows(0, 512, early, False)
    arrived("axp1")
    send_act(("ac", 5), col_at(1, -1, 0), mate)
    fisher_rows(512, 512, early, False)
    arrived("axf1")
    send_act(("ac", 7), col_at(1, 2, 0), mate)
    fisher_rows(1024, 512, early, False)
    fisher_rows(1536, 128, early, False)
    for j in (5, 7):
        arrived(("ac", j))

    @pl.loop(0, HID // 512)
    def _(n):
        fisher_rows(pl.multiple_of(n * 512, 512), 512, late, True)

    fisher_rows(1536, 128, late, True)

    for k in range(8):
        pltpu.make_async_copy(part.at[0], recv.at[k], part_recv.at[k]).wait()

    for _, copy in sent:
        copy.wait_send()
    for i, b in enumerate(dests):
        @pl.when(b != c)
        def _():
            pltpu.make_async_remote_copy(
                src_ref=part.at[i], dst_ref=recv.at[chip], send_sem=part_send.at[i],
                recv_sem=part_recv.at[chip], device_id=(r, b), device_id_type=MESH,
            ).wait_send()


def finish(fisher, recv, fisher_out, hidden_out, hidden, sems):
    height = HID // CHUNKS
    copies = [
        pltpu.make_async_copy(fisher.at[pl.ds(i * height, height)], fisher_out.at[pl.ds(i * height, height)], sems.at[i])
        for i in range(CHUNKS)
    ]
    for copy in copies:
        copy.start()
    for g in range(GROUPS):
        scales = [recv[k, TILES, :, pl.ds(g * 32, 1)].astype(jnp.float32) * (1.0 / RATE ** 2) for k in range(8)]

        for n in range(COLS):
            total = jnp.zeros((SUB, LANES), jnp.float32)
            for k in range(8):
                code = recv[k, g * COLS + n].astype(jnp.float32)
                level = jnp.log2(jnp.abs(code)) + OFFSET
                value = scales[k] * level * level
                total = total + jnp.where(code < 0, -value, value)
            hidden[pl.ds(g * SUB, SUB), pl.ds(n * LANES, LANES)] = total.astype(jnp.bfloat16)

    last = pltpu.make_async_copy(hidden, hidden_out, sems.at[CHUNKS])
    last.start()
    for copy in copies:
        copy.wait()
    last.wait()


def per_device(hidden_act, out_grad, down_weight):
    any_spec = pl.BlockSpec(memory_space=pl.ANY)
    fisher, recv = pl.pallas_call(
        kernel,
        out_shape=(
            pltpu.VMEM((HID, FEAT), jnp.float32),
            pltpu.VMEM((8, TILES + 1, SUB, LANES), jnp.bfloat16),
        ),
        in_specs=[any_spec] * 3,
        out_specs=(pl.BlockSpec(memory_space=pltpu.VMEM), pl.BlockSpec(memory_space=pltpu.VMEM)),
        scratch_shapes=[
            pltpu.VMEM((TOKENS, HID), jnp.bfloat16),
            pltpu.VMEM((TOKENS, FEAT), jnp.bfloat16),
            pltpu.VMEM((TOKENS, FEAT), jnp.bfloat16),
            pltpu.VMEM((2, HID, FEAT), jnp.bfloat16),
            pltpu.VMEM((2 * FEAT, HID), jnp.bfloat16),
            pltpu.VMEM((4 * TOK, 2 * FEAT), jnp.bfloat16),
            pltpu.VMEM((4 * TOK, HID), jnp.float32),
            pltpu.VMEM((8, TILES + 1, SUB, LANES), jnp.bfloat16),
            pltpu.SemaphoreType.DMA((len(KINDS),)),
            pltpu.SemaphoreType.DMA((len(KINDS),)),
            pltpu.SemaphoreType.DMA((8,)),
            pltpu.SemaphoreType.DMA((8,)),
            pltpu.SemaphoreType.DMA((3,)),
        ],
        compiler_params=pltpu.CompilerParams(
            collective_id=0, has_side_effects=True, vmem_limit_bytes=58300 * 1000,
        ),
        name="fused_grads",
    )(hidden_act, out_grad, down_weight)
    return pl.pallas_call(
        finish,
        out_shape=(
            jax.ShapeDtypeStruct((HID, FEAT), jnp.float32),
            jax.ShapeDtypeStruct((TOK, HID), jnp.bfloat16),
        ),
        in_specs=[any_spec, pl.BlockSpec(memory_space=pltpu.VMEM)],
        out_specs=(any_spec, any_spec),
        scratch_shapes=[pltpu.VMEM((TOK, HID), jnp.bfloat16), pltpu.SemaphoreType.DMA((CHUNKS + 1,))],
        compiler_params=pltpu.CompilerParams(vmem_limit_bytes=40 * 1000 * 1000),
        name="write_out",
    )(fisher, recv)


def solution(mesh):
    placed = (P("col", "row"), P("row", "col"), P("row", "col"))
    return jax.shard_map(
        per_device,
        mesh=mesh,
        in_specs=placed,
        out_specs=(P("row", "col"), P("col", "row")),
        check_vma=False,
    )
```

```python
import jax
import jax.numpy as jnp
from jax import lax
from jax.experimental import pallas as pl
from jax.experimental.pallas import tpu as pltpu
from jax.sharding import PartitionSpec as P

SEQ = 96
EXAMPLES = 8
MESH = pl.DeviceIdType.MESH

TOK = 48
HID = 1664
FEAT = 1024
TOKENS = 768
LANES = 128
SUB = 16
GROUPS = TOK // SUB
COLS = HID // LANES
TILES = GROUPS * COLS
CHUNKS = 8
RATE = 250.0
OFFSET = 125.0

KINDS = []


def kind(name):
    if name not in KINDS:
        KINDS.append(name)
    return KINDS.index(name)


for name in ("gz0", "gz1", "gz2", "gz3", "gy2"):
    kind(name)
for j in range(4):
    for name in ("gyp", "gym", "gyf"):
        kind((name, j))
for j in range(8):
    kind(("gc", j))
for name in ("az", "axp0", "axm0", "ax2", "axp1", "axm1", "axf1"):
    kind(name)
for j in range(8):
    kind(("ac", j))
kind("w")


def kernel(act, grad, weight, fisher, recv, act_all, grad_all, grad_mate, w_all, w_t, left, raw, part,
           send_sems, recv_sems, part_send, part_recv, local_sems):
    r, c = lax.axis_index("row"), lax.axis_index("col")
    zh, y = r // 4, r % 4
    zl, x, core = c // 8, (c // 2) % 4, c % 2
    chip = c // 2

    def row_at(dzh, dy):
        return ((zh + dzh) % 4) * 4 + (y + dy) % 4

    def col_at(dzl, dx, dcore):
        return ((zl + dzl) % 2) * 8 + ((x + dx) % 4) * 2 + (core + dcore) % 2

    mate = (r, col_at(0, 0, 1))

    barrier = pltpu.get_barrier_semaphore()
    peers = [(row_at(dzh, 0), c) for dzh in (1, 3)] + [(row_at(0, dy), c) for dy in (1, 2, 3)]
    peers += [(r, col_at(dzl, dx, dc)) for dzl in range(2) for dx in range(4) for dc in range(2) if (dzl, dx, dc) != (0, 0, 0)]
    for peer in peers:
        pl.semaphore_signal(barrier, inc=1, device_id=peer, device_id_type=MESH)

    def rows(b):
        return pl.ds(pl.multiple_of(b * TOK, TOK), TOK)

    local = [
        pltpu.make_async_copy(grad, grad_all.at[rows(r)], local_sems.at[0]),
        pltpu.make_async_copy(act, act_all.at[rows(c)], local_sems.at[1]),
        pltpu.make_async_copy(weight, w_all.at[0], local_sems.at[2]),
    ]
    for copy in local:
        copy.start()
    pl.semaphore_wait(barrier, len(peers))

    sent = []

    def send(name, src, dst, to):
        k = kind(name)
        copy = pltpu.make_async_remote_copy(
            src_ref=src, dst_ref=dst, send_sem=send_sems.at[k], recv_sem=recv_sems.at[k],
            device_id=to, device_id_type=MESH,
        )
        copy.start()
        sent.append((name, copy))

    def arrived(name):
        for n, copy in sent:
            if n == name:
                copy.wait_recv()
                return
        raise ValueError(name)

    def send_grad(name, b, to, src=None, columns=None):
        src, dst = grad_all.at[rows(b)] if src is None else src, grad_all.at[rows(b)]
        if columns is not None:
            src, dst = src.at[:, columns], dst.at[:, columns]
        send(name, src, dst, to)

    def send_act(name, b, to, src=None):
        send(name, act_all.at[rows(b)] if src is None else src, act_all.at[rows(b)], to)

    zstep = (0, -1, 1, 2)

    def to_mate(first, y_block):
        for i in range(2):
            b = ((1 - core) + 2 * i) * 4 + y_block
            send(("gc", first + i), grad_all.at[rows(b)], grad_mate.at[rows(b)], mate)

    def turn(half):
        @pl.loop(0, COLS)
        def _(n):
            at = pl.ds(pl.multiple_of(n * LANES, LANES), LANES)
            w_t[pl.ds(half * FEAT, FEAT), at] = w_all[half, at, :].T

    up, down, over = (row_at(0, 1), c), (row_at(0, -1), c), (row_at(0, 2), c)
    right, far = (r, col_at(0, 1, 0)), (r, col_at(0, 2, 0))
    back = (r, col_at(0, -1, 0))

    def multiply(first, y_blocks):
        blocks = [(core + 2 * i) * 4 + yb for yb in y_blocks for i in range(2)]
        count = len(blocks)
        for i, b in enumerate(blocks):
            left[pl.ds(i * TOK, TOK), pl.ds(0, FEAT)] = grad_all[rows(b), :]
            left[pl.ds(i * TOK, TOK), pl.ds(FEAT, FEAT)] = grad_mate[rows(b), :]

        raw[pl.ds(0, count * TOK), :] = jnp.dot(
            left[pl.ds(0, count * TOK), :], w_t[...], preferred_element_type=jnp.float32
        )

        @pl.loop(0, count)
        def _(i):
            lane = lax.broadcasted_iota(jnp.int32, (SUB, LANES), 1)
            scales = jnp.zeros((SUB, LANES), jnp.float32)
            for g in range(GROUPS):
                at = pl.ds(pl.multiple_of(i * TOK + g * SUB, SUB), SUB)
                top = jnp.max(jnp.abs(raw[at, :]), axis=1, keepdims=True)
                top = top.astype(jnp.bfloat16).astype(jnp.float32)
                inverse = jnp.where(top > 0, 1.0 / jnp.where(top > 0, top, 1.0), 0.0)
                scales = jnp.where(lane // 32 == g, top, scales)
                for n in range(COLS):
                    value = raw[at, pl.ds(n * LANES, LANES)]
                    level = jnp.abs(value) * inverse + 1e-30
                    code = jnp.exp2(RATE * level * lax.rsqrt(level) - OFFSET)
                    part[first + i, g * COLS + n] = jnp.where(value < 0, -code, code).astype(jnp.bfloat16)
            part[first + i, TILES] = scales.astype(jnp.bfloat16)

            yb = y_blocks[0] if len(y_blocks) == 1 else jnp.where(i < 2, y_blocks[0], y_blocks[1])
            b = (core + 2 * (i % 2)) * 4 + yb

            @pl.when(b == c)
            def _():
                pltpu.make_async_copy(part.at[first + i], recv.at[chip], part_recv.at[chip]).start()

            @pl.when(b != c)
            def _():
                pltpu.make_async_remote_copy(
                    src_ref=part.at[first + i], dst_ref=recv.at[chip], send_sem=part_send.at[first + i],
                    recv_sem=part_recv.at[chip], device_id=(r, b), device_id_type=MESH,
                ).start()

        return blocks

    send_grad("gz0", r, (row_at(1, 0), c), grad)
    send_grad("gz1", r, (row_at(-1, 0), c), grad)
    send_grad(("gyp", 0), r, up, grad)
    send_grad(("gym", 0), r, down, grad)
    send_grad("gy2", r, over, grad)
    send_act("axp0", c, right, act)
    send_act("axm0", c, back, act)
    send("w", weight, w_all.at[1], mate)
    send_act("ax2", c, far, act)
    send_act(("ac", 0), c, mate, act)
    local[2].wait()
    turn(0)

    half = FEAT // 2
    arrived("gz0")
    send_grad("gz2", row_at(-1, 0), (row_at(1, 0), c), columns=pl.ds(0, half))
    arrived("gz1")
    send_grad("gz3", row_at(1, 0), (row_at(-1, 0), c), columns=pl.ds(half, half))
    for j in (1, 2):
        send_grad(("gyp", j), row_at(zstep[j], 0), up)
        send_grad(("gym", j), row_at(zstep[j], 0), down)
    send_act("az", c, (r, col_at(1, 0, 0)), act)
    local[0].wait()
    local[1].wait()
    arrived("gz2")
    arrived("gz3")
    send_grad(("gyp", 3), row_at(2, 0), up)
    send_grad(("gym", 3), row_at(2, 0), down)
    to_mate(0, y)
    arrived("az")
    b = col_at(1, 0, 0)
    send_act("axp1", b, right)
    send_act("axm1", b, back)
    send_act(("ac", 1), b, mate)

    def forward_y(j):
        if j < 2:
            arrived(("gyp", j))
            send_grad(("gyf", j), row_at(zstep[j], -1), up)
        else:
            arrived(("gym", j))
            send_grad(("gyf", j), row_at(zstep[j], 1), down)

    forward_y(1)
    forward_y(2)
    arrived("w")
    turn(1)
    arrived(("gc", 0))
    arrived(("gc", 1))
    dests = multiply(0, [y])

    forward_y(3)
    for j in (0, 2, 3):
        arrived(("gyp", j))
    to_mate(2, (y - 1) % 4)
    for j in (0, 1):
        arrived(("gym", j))
    to_mate(4, (y + 1) % 4)
    arrived("axp0")
    send_act(("ac", 2), col_at(0, -1, 0), mate)
    arrived("axm0")
    send_act(("ac", 3), col_at(0, 1, 0), mate)
    arrived("ax2")
    send_act(("ac", 6), col_at(0, 2, 0), mate)
    arrived("axm1")
    b = col_at(1, 1, 0)
    send_act("axf1", b, back)
    send_act(("ac", 4), b, mate)
    for j in range(2, 6):
        arrived(("gc", j))
    dests += multiply(2, [(y - 1) % 4, (y + 1) % 4])

    arrived("gy2")
    for j in range(1, 4):
        arrived(("gyf", j))
    to_mate(6, (y + 2) % 4)
    for j in range(6, 8):
        arrived(("gc", j))
    dests += multiply(6, [(y + 2) % 4])

    early = [zl * 4 + e for e in range(4)] + [col_at(1, 0, 0) // 2, col_at(1, 1, 0) // 2]
    late = [col_at(1, 2, 0) // 2, col_at(1, 3, 0) // 2]

    def fisher_rows(start, height, examples, is_last):
        for f in range(FEAT // 256):
            at = pl.ds(start, height), pl.ds(f * 256, 256)
            total = fisher[at] if is_last else None
            for e in examples:
                tokens = pl.ds(pl.multiple_of(e * SEQ, SEQ), SEQ)
                piece = lax.dot_general(
                    act_all[tokens, pl.ds(start, height)], grad_all[tokens, pl.ds(f * 256, 256)],
                    (((0,), (0,)), ((), ())), preferred_element_type=jnp.float32,
                )
                total = piece * piece if total is None else total + piece * piece
            fisher[at] = total * (1.0 / (EXAMPLES * SEQ)) if is_last else total

    for j in (0, 1, 2, 3, 4, 6):
        arrived(("ac", j))

    fisher_rows(0, 512, early, False)
    arrived("axp1")
    send_act(("ac", 5), col_at(1, -1, 0), mate)
    fisher_rows(512, 512, early, False)
    arrived("axf1")
    send_act(("ac", 7), col_at(1, 2, 0), mate)
    fisher_rows(1024, 512, early, False)
    fisher_rows(1536, 128, early, False)
    for j in (5, 7):
        arrived(("ac", j))

    @pl.loop(0, HID // 512)
    def _(n):
        fisher_rows(pl.multiple_of(n * 512, 512), 512, late, True)

    fisher_rows(1536, 128, late, True)

    for k in range(8):
        pltpu.make_async_copy(part.at[0], recv.at[k], part_recv.at[k]).wait()

    for _, copy in sent:
        copy.wait_send()
    for i, b in enumerate(dests):
        @pl.when(b != c)
        def _():
            pltpu.make_async_remote_copy(
                src_ref=part.at[i], dst_ref=recv.at[chip], send_sem=part_send.at[i],
                recv_sem=part_recv.at[chip], device_id=(r, b), device_id_type=MESH,
            ).wait_send()


def finish(fisher, recv, fisher_out, hidden_out, hidden, sems):
    height = HID // CHUNKS
    copies = [
        pltpu.make_async_copy(fisher.at[pl.ds(i * height, height)], fisher_out.at[pl.ds(i * height, height)], sems.at[i])
        for i in range(CHUNKS)
    ]
    for copy in copies:
        copy.start()
    for g in range(GROUPS):
        scales = [recv[k, TILES, :, pl.ds(g * 32, 1)].astype(jnp.float32) * (1.0 / RATE ** 2) for k in range(8)]

        for n in range(COLS):
            total = jnp.zeros((SUB, LANES), jnp.float32)
            for k in range(8):
                code = recv[k, g * COLS + n].astype(jnp.float32)
                level = jnp.log2(jnp.abs(code)) + OFFSET
                value = scales[k] * level * level
                total = total + jnp.where(code < 0, -value, value)
            hidden[pl.ds(g * SUB, SUB), pl.ds(n * LANES, LANES)] = total.astype(jnp.bfloat16)

    last = pltpu.make_async_copy(hidden, hidden_out, sems.at[CHUNKS])
    last.start()
    for copy in copies:
        copy.wait()
    last.wait()


def per_device(hidden_act, out_grad, down_weight):
    any_spec = pl.BlockSpec(memory_space=pl.ANY)
    fisher, recv = pl.pallas_call(
        kernel,
        out_shape=(
            pltpu.VMEM((HID, FEAT), jnp.float32),
            pltpu.VMEM((8, TILES + 1, SUB, LANES), jnp.bfloat16),
        ),
        in_specs=[any_spec] * 3,
        out_specs=(pl.BlockSpec(memory_space=pltpu.VMEM), pl.BlockSpec(memory_space=pltpu.VMEM)),
        scratch_shapes=[
            pltpu.VMEM((TOKENS, HID), jnp.bfloat16),
            pltpu.VMEM((TOKENS, FEAT), jnp.bfloat16),
            pltpu.VMEM((TOKENS, FEAT), jnp.bfloat16),
            pltpu.VMEM((2, HID, FEAT), jnp.bfloat16),
            pltpu.VMEM((2 * FEAT, HID), jnp.bfloat16),
            pltpu.VMEM((4 * TOK, 2 * FEAT), jnp.bfloat16),
            pltpu.VMEM((4 * TOK, HID), jnp.float32),
            pltpu.VMEM((8, TILES + 1, SUB, LANES), jnp.bfloat16),
            pltpu.SemaphoreType.DMA((len(KINDS),)),
            pltpu.SemaphoreType.DMA((len(KINDS),)),
            pltpu.SemaphoreType.DMA((8,)),
            pltpu.SemaphoreType.DMA((8,)),
            pltpu.SemaphoreType.DMA((3,)),
        ],
        compiler_params=pltpu.CompilerParams(
            collective_id=0, has_side_effects=True, vmem_limit_bytes=58300 * 1000,
        ),
        name="fused_grads",
    )(hidden_act, out_grad, down_weight)
    return pl.pallas_call(
        finish,
        out_shape=(
            jax.ShapeDtypeStruct((HID, FEAT), jnp.float32),
            jax.ShapeDtypeStruct((TOK, HID), jnp.bfloat16),
        ),
        in_specs=[any_spec, pl.BlockSpec(memory_space=pltpu.VMEM)],
        out_specs=(any_spec, any_spec),
        scratch_shapes=[pltpu.VMEM((TOK, HID), jnp.bfloat16), pltpu.SemaphoreType.DMA((CHUNKS + 1,))],
        compiler_params=pltpu.CompilerParams(vmem_limit_bytes=40 * 1000 * 1000),
        name="write_out",
    )(fisher, recv)


def solution(mesh):
    placed = (P("col", "row"), P("row", "col"), P("row", "col"))
    return jax.shard_map(
        per_device,
        mesh=mesh,
        in_specs=placed,
        out_specs=(P("row", "col"), P("col", "row")),
        check_vma=False,
    )
```

```python
import jax
import jax.numpy as jnp
from jax import lax
from jax.experimental import pallas as pl
from jax.experimental.pallas import tpu as pltpu
from jax.sharding import PartitionSpec as P

SEQ = 96
EXAMPLES = 8
MESH = pl.DeviceIdType.MESH

TOK = 48
HID = 1664
FEAT = 1024
TOKENS = 768
LANES = 128
SUB = 16
GROUPS = TOK // SUB
COLS = HID // LANES
TILES = GROUPS * COLS
CHUNKS = 8
RATE = 250.0
OFFSET = 125.0

KINDS = []


def kind(name):
    if name not in KINDS:
        KINDS.append(name)
    return KINDS.index(name)


for name in ("gz0", "gz1", "gz2", "gz3", "gy2"):
    kind(name)
for j in range(4):
    for name in ("gyp", "gym", "gyf"):
        kind((name, j))
for j in range(8):
    kind(("gc", j))
for name in ("az", "axp0", "axm0", "ax2", "axp1", "axm1", "axf1"):
    kind(name)
for j in range(8):
    kind(("ac", j))
kind("w")


def kernel(act, grad, weight, fisher, recv, act_all, grad_all, grad_mate, w_all, w_t, left, raw, part,
           send_sems, recv_sems, part_send, part_recv, local_sems):
    r, c = lax.axis_index("row"), lax.axis_index("col")
    zh, y = r // 4, r % 4
    zl, x, core = c // 8, (c // 2) % 4, c % 2
    chip = c // 2

    def row_at(dzh, dy):
        return ((zh + dzh) % 4) * 4 + (y + dy) % 4

    def col_at(dzl, dx, dcore):
        return ((zl + dzl) % 2) * 8 + ((x + dx) % 4) * 2 + (core + dcore) % 2

    mate = (r, col_at(0, 0, 1))

    barrier = pltpu.get_barrier_semaphore()
    peers = [(row_at(dzh, 0), c) for dzh in (1, 3)] + [(row_at(0, dy), c) for dy in (1, 2, 3)]
    peers += [(r, col_at(dzl, dx, dc)) for dzl in range(2) for dx in range(4) for dc in range(2) if (dzl, dx, dc) != (0, 0, 0)]
    for peer in peers:
        pl.semaphore_signal(barrier, inc=1, device_id=peer, device_id_type=MESH)

    def rows(b):
        return pl.ds(pl.multiple_of(b * TOK, TOK), TOK)

    local = [
        pltpu.make_async_copy(grad, grad_all.at[rows(r)], local_sems.at[0]),
        pltpu.make_async_copy(act, act_all.at[rows(c)], local_sems.at[1]),
        pltpu.make_async_copy(weight, w_all.at[0], local_sems.at[2]),
    ]
    for copy in local:
        copy.start()
    pl.semaphore_wait(barrier, len(peers))

    sent = []

    def send(name, src, dst, to):
        k = kind(name)
        copy = pltpu.make_async_remote_copy(
            src_ref=src, dst_ref=dst, send_sem=send_sems.at[k], recv_sem=recv_sems.at[k],
            device_id=to, device_id_type=MESH,
        )
        copy.start()
        sent.append((name, copy))

    def arrived(name):
        for n, copy in sent:
            if n == name:
                copy.wait_recv()
                return
        raise ValueError(name)

    def send_grad(name, b, to, src=None, columns=None):
        src, dst = grad_all.at[rows(b)] if src is None else src, grad_all.at[rows(b)]
        if columns is not None:
            src, dst = src.at[:, columns], dst.at[:, columns]
        send(name, src, dst, to)

    def send_act(name, b, to, src=None):
        send(name, act_all.at[rows(b)] if src is None else src, act_all.at[rows(b)], to)

    zstep = (0, -1, 1, 2)

    def to_mate(first, y_block):
        for i in range(2):
            b = ((1 - core) + 2 * i) * 4 + y_block
            send(("gc", first + i), grad_all.at[rows(b)], grad_mate.at[rows(b)], mate)

    def turn(half):
        @pl.loop(0, COLS)
        def _(n):
            at = pl.ds(pl.multiple_of(n * LANES, LANES), LANES)
            w_t[pl.ds(half * FEAT, FEAT), at] = w_all[half, at, :].T

    up, down, over = (row_at(0, 1), c), (row_at(0, -1), c), (row_at(0, 2), c)
    right, far = (r, col_at(0, 1, 0)), (r, col_at(0, 2, 0))
    back = (r, col_at(0, -1, 0))

    def multiply(first, y_blocks):
        blocks = [(core + 2 * i) * 4 + yb for yb in y_blocks for i in range(2)]
        count = len(blocks)
        for i, b in enumerate(blocks):
            left[pl.ds(i * TOK, TOK), pl.ds(0, FEAT)] = grad_all[rows(b), :]
            left[pl.ds(i * TOK, TOK), pl.ds(FEAT, FEAT)] = grad_mate[rows(b), :]

        raw[pl.ds(0, count * TOK), :] = jnp.dot(
            left[pl.ds(0, count * TOK), :], w_t[...], preferred_element_type=jnp.float32
        )

        @pl.loop(0, count)
        def _(i):
            lane = lax.broadcasted_iota(jnp.int32, (SUB, LANES), 1)
            scales = jnp.zeros((SUB, LANES), jnp.float32)
            for g in range(GROUPS):
                at = pl.ds(pl.multiple_of(i * TOK + g * SUB, SUB), SUB)
                top = jnp.max(jnp.abs(raw[at, :]), axis=1, keepdims=True)
                top = top.astype(jnp.bfloat16).astype(jnp.float32)
                inverse = jnp.where(top > 0, 1.0 / jnp.where(top > 0, top, 1.0), 0.0)
                scales = jnp.where(lane // 32 == g, top, scales)
                for n in range(COLS):
                    value = raw[at, pl.ds(n * LANES, LANES)]
                    level = jnp.abs(value) * inverse + 1e-30
                    code = jnp.exp2(RATE * level * lax.rsqrt(level) - OFFSET)
                    part[first + i, g * COLS + n] = jnp.where(value < 0, -code, code).astype(jnp.bfloat16)
            part[first + i, TILES] = scales.astype(jnp.bfloat16)

            b = (core + 2 * i) * 4 + y_blocks[0]

            @pl.when(b == c)
            def _():
                pltpu.make_async_copy(part.at[first + i], recv.at[chip], part_recv.at[chip]).start()

            @pl.when(b != c)
            def _():
                pltpu.make_async_remote_copy(
                    src_ref=part.at[first + i], dst_ref=recv.at[chip], send_sem=part_send.at[first + i],
                    recv_sem=part_recv.at[chip], device_id=(r, b), device_id_type=MESH,
                ).start()

        return blocks

    send_grad("gz0", r, (row_at(1, 0), c), grad)
    send_grad("gz1", r, (row_at(-1, 0), c), grad)
    send_grad(("gyp", 0), r, up, grad)
    send_grad(("gym", 0), r, down, grad)
    send_grad("gy2", r, over, grad)
    send_act("axp0", c, right, act)
    send_act("axm0", c, back, act)
    send("w", weight, w_all.at[1], mate)
    send_act("ax2", c, far, act)
    send_act(("ac", 0), c, mate, act)
    local[2].wait()
    turn(0)

    half = FEAT // 2
    arrived("gz0")
    send_grad("gz2", row_at(-1, 0), (row_at(1, 0), c), columns=pl.ds(0, half))
    arrived("gz1")
    send_grad("gz3", row_at(1, 0), (row_at(-1, 0), c), columns=pl.ds(half, half))
    for j in (1, 2):
        send_grad(("gyp", j), row_at(zstep[j], 0), up)
        send_grad(("gym", j), row_at(zstep[j], 0), down)
    send_act("az", c, (r, col_at(1, 0, 0)), act)
    local[0].wait()
    local[1].wait()
    arrived("gz2")
    arrived("gz3")
    send_grad(("gyp", 3), row_at(2, 0), up)
    send_grad(("gym", 3), row_at(2, 0), down)
    to_mate(0, y)
    arrived("az")
    b = col_at(1, 0, 0)
    send_act("axp1", b, right)
    send_act("axm1", b, back)
    send_act(("ac", 1), b, mate)

    def forward_y(j):
        if j < 2:
            arrived(("gyp", j))
            send_grad(("gyf", j), row_at(zstep[j], -1), up)
        else:
            arrived(("gym", j))
            send_grad(("gyf", j), row_at(zstep[j], 1), down)

    forward_y(1)
    forward_y(2)
    arrived("w")
    turn(1)
    arrived(("gc", 0))
    arrived(("gc", 1))
    dests = multiply(0, [y])

    forward_y(3)
    for j in (0, 2, 3):
        arrived(("gyp", j))
    to_mate(2, (y - 1) % 4)
    for j in (0, 1):
        arrived(("gym", j))
    to_mate(4, (y + 1) % 4)
    arrived("axp0")
    send_act(("ac", 2), col_at(0, -1, 0), mate)
    arrived("axm0")
    send_act(("ac", 3), col_at(0, 1, 0), mate)
    arrived("ax2")
    send_act(("ac", 6), col_at(0, 2, 0), mate)
    arrived("axm1")
    b = col_at(1, 1, 0)
    send_act("axf1", b, back)
    send_act(("ac", 4), b, mate)
    for j in (2, 3):
        arrived(("gc", j))
    dests += multiply(2, [(y - 1) % 4])
    for j in (4, 5):
        arrived(("gc", j))
    dests += multiply(4, [(y + 1) % 4])

    arrived("gy2")
    for j in range(1, 4):
        arrived(("gyf", j))
    to_mate(6, (y + 2) % 4)
    for j in range(6, 8):
        arrived(("gc", j))
    dests += multiply(6, [(y + 2) % 4])

    early = [zl * 4 + e for e in range(4)] + [col_at(1, 0, 0) // 2, col_at(1, 1, 0) // 2]
    late = [col_at(1, 2, 0) // 2, col_at(1, 3, 0) // 2]

    def fisher_rows(start, height, examples, is_last):
        for f in range(FEAT // 256):
            at = pl.ds(start, height), pl.ds(f * 256, 256)
            total = fisher[at] if is_last else None
            for e in examples:
                tokens = pl.ds(pl.multiple_of(e * SEQ, SEQ), SEQ)
                piece = lax.dot_general(
                    act_all[tokens, pl.ds(start, height)], grad_all[tokens, pl.ds(f * 256, 256)],
                    (((0,), (0,)), ((), ())), preferred_element_type=jnp.float32,
                )
                total = piece * piece if total is None else total + piece * piece
            fisher[at] = total * (1.0 / (EXAMPLES * SEQ)) if is_last else total

    for j in (0, 1, 2, 3, 4, 6):
        arrived(("ac", j))

    fisher_rows(0, 512, early, False)
    arrived("axp1")
    send_act(("ac", 5), col_at(1, -1, 0), mate)
    fisher_rows(512, 512, early, False)
    arrived("axf1")
    send_act(("ac", 7), col_at(1, 2, 0), mate)
    fisher_rows(1024, 512, early, False)
    fisher_rows(1536, 128, early, False)
    for j in (5, 7):
        arrived(("ac", j))

    @pl.loop(0, HID // 512)
    def _(n):
        fisher_rows(pl.multiple_of(n * 512, 512), 512, late, True)

    fisher_rows(1536, 128, late, True)

    for k in range(8):
        pltpu.make_async_copy(part.at[0], recv.at[k], part_recv.at[k]).wait()

    for _, copy in sent:
        copy.wait_send()
    for i, b in enumerate(dests):
        @pl.when(b != c)
        def _():
            pltpu.make_async_remote_copy(
                src_ref=part.at[i], dst_ref=recv.at[chip], send_sem=part_send.at[i],
                recv_sem=part_recv.at[chip], device_id=(r, b), device_id_type=MESH,
            ).wait_send()


def finish(fisher, recv, fisher_out, hidden_out, hidden, sems):
    height = HID // CHUNKS
    copies = [
        pltpu.make_async_copy(fisher.at[pl.ds(i * height, height)], fisher_out.at[pl.ds(i * height, height)], sems.at[i])
        for i in range(CHUNKS)
    ]
    for copy in copies:
        copy.start()
    for g in range(GROUPS):
        scales = [recv[k, TILES, :, pl.ds(g * 32, 1)].astype(jnp.float32) * (1.0 / RATE ** 2) for k in range(8)]

        for n in range(COLS):
            total = jnp.zeros((SUB, LANES), jnp.float32)
            for k in range(8):
                code = recv[k, g * COLS + n].astype(jnp.float32)
                level = jnp.log2(jnp.abs(code)) + OFFSET
                value = scales[k] * level * level
                total = total + jnp.where(code < 0, -value, value)
            hidden[pl.ds(g * SUB, SUB), pl.ds(n * LANES, LANES)] = total.astype(jnp.bfloat16)

    last = pltpu.make_async_copy(hidden, hidden_out, sems.at[CHUNKS])
    last.start()
    for copy in copies:
        copy.wait()
    last.wait()


def per_device(hidden_act, out_grad, down_weight):
    any_spec = pl.BlockSpec(memory_space=pl.ANY)
    fisher, recv = pl.pallas_call(
        kernel,
        out_shape=(
            pltpu.VMEM((HID, FEAT), jnp.float32),
            pltpu.VMEM((8, TILES + 1, SUB, LANES), jnp.bfloat16),
        ),
        in_specs=[any_spec] * 3,
        out_specs=(pl.BlockSpec(memory_space=pltpu.VMEM), pl.BlockSpec(memory_space=pltpu.VMEM)),
        scratch_shapes=[
            pltpu.VMEM((TOKENS, HID), jnp.bfloat16),
            pltpu.VMEM((TOKENS, FEAT), jnp.bfloat16),
            pltpu.VMEM((TOKENS, FEAT), jnp.bfloat16),
            pltpu.VMEM((2, HID, FEAT), jnp.bfloat16),
            pltpu.VMEM((2 * FEAT, HID), jnp.bfloat16),
            pltpu.VMEM((4 * TOK, 2 * FEAT), jnp.bfloat16),
            pltpu.VMEM((4 * TOK, HID), jnp.float32),
            pltpu.VMEM((8, TILES + 1, SUB, LANES), jnp.bfloat16),
            pltpu.SemaphoreType.DMA((len(KINDS),)),
            pltpu.SemaphoreType.DMA((len(KINDS),)),
            pltpu.SemaphoreType.DMA((8,)),
            pltpu.SemaphoreType.DMA((8,)),
            pltpu.SemaphoreType.DMA((3,)),
        ],
        compiler_params=pltpu.CompilerParams(
            collective_id=0, has_side_effects=True, vmem_limit_bytes=58300 * 1000,
        ),
        name="fused_grads",
    )(hidden_act, out_grad, down_weight)
    return pl.pallas_call(
        finish,
        out_shape=(
            jax.ShapeDtypeStruct((HID, FEAT), jnp.float32),
            jax.ShapeDtypeStruct((TOK, HID), jnp.bfloat16),
        ),
        in_specs=[any_spec, pl.BlockSpec(memory_space=pltpu.VMEM)],
        out_specs=(any_spec, any_spec),
        scratch_shapes=[pltpu.VMEM((TOK, HID), jnp.bfloat16), pltpu.SemaphoreType.DMA((CHUNKS + 1,))],
        compiler_params=pltpu.CompilerParams(vmem_limit_bytes=40 * 1000 * 1000),
        name="write_out",
    )(fisher, recv)


def solution(mesh):
    placed = (P("col", "row"), P("row", "col"), P("row", "col"))
    return jax.shard_map(
        per_device,
        mesh=mesh,
        in_specs=placed,
        out_specs=(P("row", "col"), P("col", "row")),
        check_vma=False,
    )
```
